1024 devices in a mesh: row: 32 (over z, y_lo, core), col: 32 (over x, y_hi).
Axes of the slice: x: 8, y: 8 (y_hi: 4, y_lo: 2; y = y_hi * 2 + y_lo), z: 8, core: 2. Of those that a mesh axis runs over, the one named last changes fastest.
Arguments:
- left_blocks: bfloat16 [32, 576, 128, 128], P('row', 'col')
- left_slots: int32 [32, 576], P('row', 'col'), may hold values from 0 to 36, as said below
- right_blocks: bfloat16 [32, 576, 128, 128], P('row', 'col')
- right_slots: int32 [32, 576], P('row', 'col'), may hold values from 0 to 36, as said below
Outputs:
- product_window: bfloat16 [24576, 24576], P('row', 'col')
- trace_scaled: float32 [], replicated
- norm_scaled: float32 [], replicated
The draws below stay inside these ranges and needn't reach their ends.
Inputs may be any that keep to these rules, and one draw needn't show every extreme that they name: `left_slots`: in each tile the live entries come first, are distinct and lie below 36; the others equal 36 and mark empty slots. Every tile has one live slot or more, and in every draw some tile has all 18 slots live. `right_slots`: as for left_slots.
All inputs are finite; a program needn't handle non-finite values.
Results may differ from the reference program's by a relative error of at most 0.001.
Values may be sent and summed in bfloat16 or wider, within the bound.
No kernel may reach another device: no remote copies, remote signals or barrier semaphores. Data moves between devices by JAX's collectives and lax.ppermute only.
A program may use at most 32 MiB of HBM per device.

```python
import math
import jax
import jax.numpy as jnp
from jax import lax

BLK = 128
TB = 6
STEPS = 4
SLOTS = 18
TILE = 768
N_ROW = 32
N_COL = 32


def slot_table(key):
    tile_count = N_ROW * N_COL
    cell_count = TB * TB
    key_rank, key_one, key_two, key_full = jax.random.split(key, 4)
    scores = jax.random.randint(key_rank, (tile_count, cell_count), 0, 1048576) * cell_count + jnp.arange(cell_count, dtype=jnp.int32)[None, :]
    ranking = jnp.argsort(scores, axis=1, stable=True).astype(jnp.int32)
    chosen = ranking[:, :SLOTS]
    draw_one = jax.random.randint(key_one, (tile_count,), 1, SLOTS + 1)
    draw_two = jax.random.randint(key_two, (tile_count,), 1, SLOTS + 1)
    live_count = jnp.maximum(1, draw_one * draw_two // SLOTS)
    full_tile = jax.random.randint(key_full, (), 0, tile_count)
    live_count = jnp.where(jnp.arange(tile_count, dtype=jnp.int32) == full_tile, SLOTS, live_count)
    slot_rank = jnp.arange(SLOTS, dtype=jnp.int32)[None, :]
    slot_map = jnp.where(slot_rank < live_count[:, None], chosen, cell_count)
    return slot_map.reshape(N_ROW, N_COL * SLOTS).astype(jnp.int32)


def draw_left_slots(key, part):
    key = jax.random.fold_in(key, 21)
    return slot_table(key)


def draw_right_slots(key, part):
    key = jax.random.fold_in(key, 22)
    return slot_table(key)


def draw_left_blocks(key, part):
    key = jax.random.fold_in(key, 11)
    key_values, key_scale = jax.random.split(key, 2)
    full_shape = (N_ROW, N_COL * SLOTS, BLK, BLK)
    entries = jax.random.normal(key_values, full_shape, jnp.float32)
    row_scale = jnp.exp(jax.random.uniform(key_scale, (N_ROW, N_COL * SLOTS, BLK, 1), jnp.float32, math.log(0.3), math.log(3.0)))
    rising = 3.0 ** (jnp.arange(N_ROW, dtype=jnp.float32) / max(N_ROW - 1, 1))
    return (0.2 * entries * row_scale * rising[:, None, None, None]).astype(jnp.bfloat16)


def draw_right_blocks(key, part):
    key = jax.random.fold_in(key, 12)
    key_values, key_scale = jax.random.split(key, 2)
    full_shape = (N_ROW, N_COL * SLOTS, BLK, BLK)
    entries = jax.random.normal(key_values, full_shape, jnp.float32)
    col_scale = jnp.exp(jax.random.uniform(key_scale, (N_ROW, N_COL * SLOTS, 1, BLK), jnp.float32, math.log(0.3), math.log(3.0)))
    return (0.2 * entries * col_scale).astype(jnp.bfloat16)


def setup_inputs(seed: int = 0) -> dict:
    arg_keys = jax.random.split(jax.random.key(seed), 5)
    return {
        "left_blocks": draw_left_blocks(jax.random.fold_in(arg_keys[4], 71), 0),
        "left_slots": draw_left_slots(jax.random.fold_in(arg_keys[4], 71), 0),
        "right_blocks": draw_right_blocks(jax.random.fold_in(arg_keys[4], 71), 0),
        "right_slots": draw_right_slots(jax.random.fold_in(arg_keys[4], 71), 0),
    }


def densify(blocks, positions):
    cell_count = TB * TB
    onehot = (jnp.arange(cell_count, dtype=jnp.int32)[:, None] == positions[None, :]).astype(jnp.float32)
    placed = jnp.einsum('ps,sab->pab', onehot, blocks.astype(jnp.float32)).astype(jnp.bfloat16)
    return placed.reshape(TB, TB, BLK, BLK).transpose(0, 2, 1, 3).reshape(TB * BLK, TB * BLK)

def reference(left_blocks, left_slots, right_blocks, right_slots):
    left_tiles = left_blocks.reshape(N_ROW, N_COL, SLOTS, BLK, BLK)
    left_cells = left_slots.reshape(N_ROW, N_COL, SLOTS)
    right_tiles = right_blocks.reshape(N_ROW, N_COL, SLOTS, BLK, BLK)
    right_cells = right_slots.reshape(N_ROW, N_COL, SLOTS)

    def one_tile(tile_index):
        row_index = tile_index // N_COL
        col_index = tile_index % N_COL
        running = jnp.zeros((TILE, TILE), jnp.float32)
        for step in range(STEPS):
            left_col = (col_index + step) % N_COL
            right_row = (row_index + step) % N_ROW
            left_matrix = densify(left_tiles[row_index, left_col], left_cells[row_index, left_col])
            right_matrix = densify(right_tiles[right_row, col_index], right_cells[right_row, col_index])
            running = running + jnp.dot(left_matrix, right_matrix, preferred_element_type=jnp.float32)
        trace_part = jnp.trace(running)
        diagonal_sum = jnp.where(row_index == col_index, trace_part, jnp.zeros_like(trace_part))
        return (running.astype(jnp.bfloat16), diagonal_sum, jnp.sum(running * running))
    tiles, diagonals, squares = lax.map(one_tile, jnp.arange(N_ROW * N_COL, dtype=jnp.int32))
    product_window = tiles.reshape(N_ROW, N_COL, TILE, TILE).transpose(0, 2, 1, 3).reshape(N_ROW * TILE, N_COL * TILE)
    trace_scaled = jnp.sum(diagonals) / math.sqrt(min(N_ROW, N_COL) * TILE)
    norm_scaled = jnp.sum(squares) / (N_ROW * N_COL * TILE * TILE)
    return (product_window, trace_scaled, norm_scaled)
```

```python
import functools
import math

import jax
import jax.numpy as jnp
from jax import lax
from jax.experimental import pallas as pl
from jax.experimental.pallas import tpu as pltpu
from jax.sharding import PartitionSpec as P

BLK = 128
TB = 6
STEPS = 4
TILE = TB * BLK
TAIL = 16
LANES = 128
BOTH = ("row", "col")


def pack_kernel(left_slots, right_slots, left, right, left_out, right_out, rows, sems):
    depth = left.shape[0]
    copies = [
        pltpu.make_async_copy(left, left_out.at[pl.ds(0, depth)], sems.at[0]),
        pltpu.make_async_copy(right, right_out.at[pl.ds(0, depth)], sems.at[1]),
    ]
    for copy in copies:
        copy.start()
    lane = lax.broadcasted_iota(jnp.int32, (TAIL, LANES), 1)
    for side, slots in enumerate((left_slots, right_slots)):
        cells = jnp.zeros((TAIL, LANES), jnp.int32)
        for slot in range(slots.shape[1]):
            cells = jnp.where(lane == slot, slots[0, slot], cells)
        rows[side] = cells.astype(jnp.float32).astype(jnp.bfloat16)
    tails = [
        pltpu.make_async_copy(rows.at[0], left_out.at[pl.ds(depth, TAIL)], sems.at[2]),
        pltpu.make_async_copy(rows.at[1], right_out.at[pl.ds(depth, TAIL)], sems.at[3]),
    ]
    for copy in tails:
        copy.start()
    for copy in copies + tails:
        copy.wait()


def pack(left_slots, right_slots, left, right):
    depth = left.shape[0]
    packed = jax.ShapeDtypeStruct((depth + TAIL, LANES), left.dtype)
    return pl.pallas_call(
        pack_kernel,
        out_shape=(packed, packed),
        in_specs=[pl.BlockSpec(memory_space=pltpu.SMEM)] * 2 + [pl.BlockSpec(memory_space=pl.ANY)] * 2,
        out_specs=(pl.BlockSpec(memory_space=pl.ANY),) * 2,
        scratch_shapes=[pltpu.VMEM((2, TAIL, LANES), left.dtype), pltpu.SemaphoreType.DMA((4,))],
        name="pack_tiles",
    )(left_slots, right_slots, left, right)


def multiply_kernel(on_diagonal, *refs):
    tiles, (out, sums, left_dense, right_dense, cells, table, sem) = refs[: 2 * STEPS], refs[2 * STEPS :]
    depth = tiles[0].shape[0] - TAIL
    slots = depth // BLK
    level = lax.broadcasted_iota(jnp.int32, (8, LANES), 0)
    gathered = jnp.zeros((8, LANES), jnp.int32)
    for index, tile in enumerate(tiles):
        tail = tile[depth : depth + TAIL, :].astype(jnp.float32).astype(jnp.int32)
        gathered = jnp.where(level == index, tail[0:8], gathered)
    cells[...] = gathered
    copy = pltpu.make_async_copy(cells, table, sem)
    copy.start()
    left_dense[...] = jnp.zeros_like(left_dense)
    right_dense[...] = jnp.zeros_like(right_dense)
    copy.wait()
    for step in range(STEPS):
        left, right = tiles[2 * step], tiles[2 * step + 1]
        for slot in range(slots):
            cell = table[2 * step, slot]
            row = pl.multiple_of(cell // TB * BLK, BLK)
            col = pl.multiple_of(step * TILE + cell % TB * BLK, BLK)
            left_dense[pl.ds(row, BLK), pl.ds(col, BLK)] = left[slot * BLK : (slot + 1) * BLK, :]
            cell = table[2 * step + 1, slot]
            row = jnp.where(cell < TB * TB, step * TILE + cell // TB * BLK, STEPS * TILE)
            row = pl.multiple_of(row, BLK)
            col = pl.multiple_of(cell % TB * BLK, BLK)
            right_dense[pl.ds(row, BLK), pl.ds(col, BLK)] = right[slot * BLK : (slot + 1) * BLK, :]
    width = 2 * BLK
    square_sum = jnp.float32(0)
    diagonal_sum = jnp.float32(0)
    inside = lax.broadcasted_iota(jnp.int32, (width, width), 0) == lax.broadcasted_iota(
        jnp.int32, (width, width), 1
    )
    for part in range(TILE // width):
        low, high = part * width, (part + 1) * width
        accum = jnp.dot(
            left_dense[0:TILE, :],
            right_dense[0 : STEPS * TILE, low:high],
            preferred_element_type=jnp.float32,
        )
        out[:, low:high] = accum.astype(out.dtype)
        square_sum += jnp.sum(accum * accum)
        diagonal_sum += jnp.sum(jnp.where(inside, accum[low:high, :], 0.0))
    diagonal_sum = jnp.where(on_diagonal[0] > 0, diagonal_sum, 0.0)
    lane = lax.broadcasted_iota(jnp.int32, sums.shape, 1)
    sums[...] = jnp.where(lane == 0, diagonal_sum, jnp.where(lane == 1, square_sum, 0.0))


def multiply(on_diagonal, tiles, fan):
    whole = pl.BlockSpec(memory_space=pltpu.VMEM)
    return pl.pallas_call(
        multiply_kernel,
        out_shape=(
            jax.ShapeDtypeStruct((TILE, TILE), jnp.bfloat16),
            jax.ShapeDtypeStruct((fan, LANES), jnp.float32),
        ),
        in_specs=[pl.BlockSpec(memory_space=pltpu.SMEM)] + [whole] * len(tiles),
        out_specs=(whole, whole),
        scratch_shapes=[
            pltpu.VMEM((TILE + BLK, STEPS * TILE), jnp.bfloat16),
            pltpu.VMEM((STEPS * TILE + BLK, TILE), jnp.bfloat16),
            pltpu.VMEM((8, LANES), jnp.int32),
            pltpu.SMEM((8, LANES), jnp.int32),
            pltpu.SemaphoreType.DMA,
        ],
        compiler_params=pltpu.CompilerParams(vmem_limit_bytes=40 * 2**20),
        cost_estimate=pl.CostEstimate(
            flops=2 * STEPS * TILE**3, bytes_accessed=8 * 600_000 + 2 * TILE * TILE, transcendentals=0
        ),
        name="place_and_multiply",
    )(on_diagonal, *tiles)


def exchange(value, target, rows, cols):
    pairs = []
    for i in range(rows):
        for j in range(cols):
            to_row, to_col = target(i, j)
            pairs.append((i * cols + j, to_row % rows * cols + to_col % cols))
    return lax.ppermute(value, BOTH, pairs)


def spread_sum(values, axis):
    return lax.all_to_all(values, axis, 0, 0, tiled=True)


def body(left_blocks, left_slots, right_blocks, right_slots):
    rows, cols = lax.axis_size("row"), lax.axis_size("col")
    on_diagonal = (lax.axis_index("row") == lax.axis_index("col")).astype(jnp.int32).reshape(1)
    left, right = pack(
        left_slots, right_slots, left_blocks.reshape(-1, LANES), right_blocks.reshape(-1, LANES)
    )
    move = functools.partial(exchange, rows=rows, cols=cols)
    left_first = move(left, lambda i, j: (i, j - 1 if i % 2 == 0 else j - 3))
    left_second = move(left, lambda i, j: (i, j - 3 if i % 2 == 0 else j - 1))
    left_middle = move(left_first, lambda i, j: (i, j - 1 if i % 2 == 0 else j + 1))
    right_middle = move(right, lambda i, j: (i - 2, j))
    right_first = move(right, lambda i, j: (i - 1 if i % 2 else i - 3, j))
    right_second = move(right_middle, lambda i, j: (i ^ 1, j))
    tiles = (left, right, left_first, right_first, left_second, right_second, left_middle, right_middle)
    product, partial = multiply(on_diagonal, tiles, rows)
    row_sums = jnp.sum(spread_sum(partial, "row"), axis=0, keepdims=True)
    totals = jnp.sum(spread_sum(jnp.broadcast_to(row_sums, (cols, LANES)), "col"), axis=0)
    trace_scaled = totals[0] / math.sqrt(min(rows, cols) * TILE)
    norm_scaled = totals[1] / (rows * cols * TILE * TILE)
    return product, trace_scaled, norm_scaled


def solution(mesh):
    placed = (
        P("row", "col", None, None),
        P("row", "col"),
        P("row", "col", None, None),
        P("row", "col"),
    )
    return jax.shard_map(
        body, mesh=mesh, in_specs=placed, out_specs=(P("row", "col"), P(), P()), check_vma=False
    )
```

```python
import functools
import math

import jax
import jax.numpy as jnp
from jax import lax
from jax.experimental import pallas as pl
from jax.experimental.pallas import tpu as pltpu
from jax.sharding import PartitionSpec as P

BLK = 128
TB = 6
STEPS = 4
TILE = TB * BLK
TAIL = 16
LANES = 128
BOTH = ("row", "col")


def pack_kernel(left_slots, right_slots, left, right, left_out, right_out, sems):
    depth = left.shape[0]
    sides = ((left_slots, left, left_out), (right_slots, right, right_out))
    copies = []
    for side, (_, source, out) in enumerate(sides):
        copies.append(pltpu.make_async_copy(source, out.at[pl.ds(0, depth)], sems.at[side]))
        copies[-1].start()
    lane = lax.broadcasted_iota(jnp.int32, (TAIL, LANES), 1)
    for slots, _, out in sides:
        cells = jnp.zeros((TAIL, LANES), jnp.int32)
        for slot in range(slots.shape[1]):
            cells = jnp.where(lane == slot, slots[0, slot], cells)
        out[depth : depth + TAIL, :] = cells.astype(jnp.float32).astype(out.dtype)
    for copy in copies:
        copy.wait()


def pack(left_slots, right_slots, left, right):
    depth = left.shape[0]
    packed = jax.ShapeDtypeStruct((depth + TAIL, LANES), left.dtype)
    return pl.pallas_call(
        pack_kernel,
        out_shape=(packed, packed),
        in_specs=[pl.BlockSpec(memory_space=pltpu.SMEM)] * 2 + [pl.BlockSpec(memory_space=pl.ANY)] * 2,
        out_specs=(pl.BlockSpec(memory_space=pltpu.VMEM),) * 2,
        scratch_shapes=[pltpu.SemaphoreType.DMA((2,))],
        name="pack_tiles",
    )(left_slots, right_slots, left, right)


def gather_cells(tiles, cells, table, sem):
    depth = tiles[0].shape[0] - TAIL
    level = lax.broadcasted_iota(jnp.int32, cells.shape, 0)
    gathered = jnp.zeros(cells.shape, jnp.int32)
    for index, tile in enumerate(tiles):
        tail = tile[depth : depth + TAIL, :].astype(jnp.float32).astype(jnp.int32)
        gathered = jnp.where(level == index, tail[0 : cells.shape[0]], gathered)
    cells[...] = gathered
    copy = pltpu.make_async_copy(cells, table, sem)
    copy.start()
    return copy


def place(tile, table, index, dense, base, side):
    for slot in range((tile.shape[0] - TAIL) // BLK):
        cell = table[index, slot]
        row, col = cell // TB * BLK, cell % TB * BLK
        if side == "left":
            col = base + col
        else:
            row = jnp.where(cell < TB * TB, base + row, dense.shape[0] - BLK)
        row, col = pl.multiple_of(row, BLK), pl.multiple_of(col, BLK)
        dense[pl.ds(row, BLK), pl.ds(col, BLK)] = tile[slot * BLK : (slot + 1) * BLK, :]


def early_kernel(left_0, right_0, left_1, right_1, right_2, right_3, accum, later, left_dense, right_dense, cells, table, sem):
    tiles = (left_0, right_0, left_1, right_1, right_2, right_3)
    copy = gather_cells(tiles, cells, table, sem)
    for dense in (left_dense, right_dense, later):
        dense[...] = jnp.zeros_like(dense)
    copy.wait()
    place(left_0, table, 0, left_dense, 0, "left")
    place(right_0, table, 1, right_dense, 0, "right")
    place(left_1, table, 2, left_dense, TILE, "left")
    place(right_1, table, 3, right_dense, TILE, "right")
    place(right_2, table, 4, later, 0, "right")
    place(right_3, table, 5, later, TILE, "right")
    for low in range(0, TILE, 2 * BLK):
        accum[:, low : low + 2 * BLK] = jnp.dot(
            left_dense[0:TILE, :],
            right_dense[0 : 2 * TILE, low : low + 2 * BLK],
            preferred_element_type=jnp.float32,
        )


def late_kernel(on_diagonal, accum, right_dense, left_2, left_3, out, sums, left_dense, cells, table, sem):
    copy = gather_cells((left_2, left_3), cells, table, sem)
    left_dense[...] = jnp.zeros_like(left_dense)
    copy.wait()
    place(left_2, table, 0, left_dense, 0, "left")
    place(left_3, table, 1, left_dense, TILE, "left")
    width = 2 * BLK
    square_sum = jnp.float32(0)
    diagonal_sum = jnp.float32(0)
    inside = lax.broadcasted_iota(jnp.int32, (width, width), 0) == lax.broadcasted_iota(
        jnp.int32, (width, width), 1
    )
    for low in range(0, TILE, width):
        total = accum[:, low : low + width] + jnp.dot(
            left_dense[0:TILE, :],
            right_dense[0 : 2 * TILE, low : low + width],
            preferred_element_type=jnp.float32,
        )
        out[:, low : low + width] = total.astype(out.dtype)
        square_sum += jnp.sum(total * total)
        diagonal_sum += jnp.sum(jnp.where(inside, total[low : low + width, :], 0.0))
    diagonal_sum = jnp.where(on_diagonal[0] > 0, diagonal_sum, 0.0)
    lane = lax.broadcasted_iota(jnp.int32, sums.shape, 1)
    sums[...] = jnp.where(lane == 0, diagonal_sum, jnp.where(lane == 1, square_sum, 0.0))


WHOLE = pl.BlockSpec(memory_space=pltpu.VMEM)
LEFT_PAIR = pltpu.VMEM((TILE + BLK, 2 * TILE), jnp.bfloat16)
RIGHT_PAIR = (2 * TILE + BLK, TILE)
CELLS = [pltpu.VMEM((8, LANES), jnp.int32), pltpu.SMEM((8, LANES), jnp.int32), pltpu.SemaphoreType.DMA]


def multiply_early(tiles):
    return pl.pallas_call(
        early_kernel,
        out_shape=(
            jax.ShapeDtypeStruct((TILE, TILE), jnp.float32),
            jax.ShapeDtypeStruct(RIGHT_PAIR, jnp.bfloat16),
        ),
        in_specs=[WHOLE] * len(tiles),
        out_specs=(WHOLE, WHOLE),
        scratch_shapes=[LEFT_PAIR, pltpu.VMEM(RIGHT_PAIR, jnp.bfloat16)] + CELLS,
        compiler_params=pltpu.CompilerParams(vmem_limit_bytes=24 * 2**20),
        cost_estimate=pl.CostEstimate(flops=4 * TILE**3, bytes_accessed=10_000_000, transcendentals=0),
        name="first_two_products",
    )(*tiles)


def multiply_late(on_diagonal, accum, right_dense, tiles, fan):
    return pl.pallas_call(
        late_kernel,
        out_shape=(
            jax.ShapeDtypeStruct((TILE, TILE), jnp.bfloat16),
            jax.ShapeDtypeStruct((fan, LANES), jnp.float32),
        ),
        in_specs=[pl.BlockSpec(memory_space=pltpu.SMEM)] + [WHOLE] * 4,
        out_specs=(WHOLE, WHOLE),
        scratch_shapes=[LEFT_PAIR] + CELLS,
        compiler_params=pltpu.CompilerParams(vmem_limit_bytes=24 * 2**20),
        cost_estimate=pl.CostEstimate(flops=4 * TILE**3, bytes_accessed=8_000_000, transcendentals=0),
        name="last_two_products",
    )(on_diagonal, accum, right_dense, *tiles)


def exchange(value, target, rows, cols):
    pairs = []
    for i in range(rows):
        for j in range(cols):
            to_row, to_col = target(i, j)
            pairs.append((i * cols + j, to_row % rows * cols + to_col % cols))
    return lax.ppermute(value, BOTH, pairs)


def spread_sum(values, axis):
    return lax.all_to_all(values, axis, 0, 0, tiled=True)


def body(left_blocks, left_slots, right_blocks, right_slots):
    rows, cols = lax.axis_size("row"), lax.axis_size("col")
    on_diagonal = (lax.axis_index("row") == lax.axis_index("col")).astype(jnp.int32).reshape(1)
    left, right = pack(
        left_slots, right_slots, left_blocks.reshape(-1, LANES), right_blocks.reshape(-1, LANES)
    )
    move = functools.partial(exchange, rows=rows, cols=cols)
    right_middle = move(right, lambda i, j: (i - 2, j))
    left_first = move(left, lambda i, j: (i, j - 1 if i % 2 == 0 else j - 3))
    left_second = move(left, lambda i, j: (i, j - 3 if i % 2 == 0 else j - 1))
    left_middle = move(left_first, lambda i, j: (i, j - 1 if i % 2 == 0 else j + 1))
    right_first = move(right, lambda i, j: (i - 1 if i % 2 else i - 3, j))
    right_second = move(right_middle, lambda i, j: (i ^ 1, j))
    accum, later = multiply_early((left, right, left_first, right_first, right_second, right_middle))
    product, partial = multiply_late(on_diagonal, accum, later, (left_second, left_middle), rows)
    row_sums = jnp.sum(spread_sum(partial, "row"), axis=0, keepdims=True)
    totals = jnp.sum(spread_sum(jnp.broadcast_to(row_sums, (cols, LANES)), "col"), axis=0)
    trace_scaled = totals[0] / math.sqrt(min(rows, cols) * TILE)
    norm_scaled = totals[1] / (rows * cols * TILE * TILE)
    return product, trace_scaled, norm_scaled


def solution(mesh):
    placed = (
        P("row", "col", None, None),
        P("row", "col"),
        P("row", "col", None, None),
        P("row", "col"),
    )
    return jax.shard_map(
        body, mesh=mesh, in_specs=placed, out_specs=(P("row", "col"), P(), P()), check_vma=False
    )
```

```python
import functools
import math

import jax
import jax.numpy as jnp
from jax import lax
from jax.experimental import pallas as pl
from jax.experimental.pallas import tpu as pltpu
from jax.sharding import PartitionSpec as P

BLK = 128
TB = 6
STEPS = 4
TILE = TB * BLK
TAIL = 16
LANES = 128
BOTH = ("row", "col")


def pack_kernel(left_slots, right_slots, left, right, left_out, right_out, sems):
    depth = left.shape[0]
    sides = ((left_slots, left, left_out), (right_slots, right, right_out))
    copies = []
    for side, (_, source, out) in enumerate(sides):
        copies.append(pltpu.make_async_copy(source, out.at[pl.ds(0, depth)], sems.at[side]))
        copies[-1].start()
    lane = lax.broadcasted_iota(jnp.int32, (TAIL, LANES), 1)
    for slots, _, out in sides:
        cells = jnp.zeros((TAIL, LANES), jnp.int32)
        for slot in range(slots.shape[1]):
            cells = jnp.where(lane == slot, slots[0, slot], cells)
        out[depth : depth + TAIL, :] = cells.astype(jnp.float32).astype(out.dtype)
    for copy in copies:
        copy.wait()


def pack(left_slots, right_slots, left, right):
    depth = left.shape[0]
    packed = jax.ShapeDtypeStruct((depth + TAIL, LANES), left.dtype)
    return pl.pallas_call(
        pack_kernel,
        out_shape=(packed, packed),
        in_specs=[pl.BlockSpec(memory_space=pltpu.SMEM)] * 2 + [pl.BlockSpec(memory_space=pl.ANY)] * 2,
        out_specs=(pl.BlockSpec(memory_space=pltpu.VMEM),) * 2,
        scratch_shapes=[pltpu.SemaphoreType.DMA((2,))],
        compiler_params=pltpu.CompilerParams(vmem_limit_bytes=4 * 2**20),
        name="pack_tiles",
    )(left_slots, right_slots, left, right)


def gather_cells(tiles, cells, table, sem):
    depth = tiles[0].shape[0] - TAIL
    level = lax.broadcasted_iota(jnp.int32, cells.shape, 0)
    gathered = jnp.zeros(cells.shape, jnp.int32)
    for index, tile in enumerate(tiles):
        tail = tile[depth : depth + TAIL, :].astype(jnp.float32).astype(jnp.int32)
        gathered = jnp.where(level == index, tail[0 : cells.shape[0]], gathered)
    cells[...] = gathered
    copy = pltpu.make_async_copy(cells, table, sem)
    copy.start()
    return copy


def place(tile, table, index, dense, base, side):
    for slot in range((tile.shape[0] - TAIL) // BLK):
        cell = table[index, slot]
        row, col = cell // TB * BLK, cell % TB * BLK
        if side == "left":
            col = base + col
        else:
            row = jnp.where(cell < TB * TB, base + row, dense.shape[0] - BLK)
        row, col = pl.multiple_of(row, BLK), pl.multiple_of(col, BLK)
        dense[pl.ds(row, BLK), pl.ds(col, BLK)] = tile[slot * BLK : (slot + 1) * BLK, :]


def early_kernel(left_0, right_0, left_1, right_1, left_2, right_2, right_3, accum, later, left_dense, right_dense, cells, table, sem):
    tiles = (left_0, right_0, left_1, right_1, left_2, right_2)
    copy = gather_cells(tiles + (right_3,), cells, table, sem)
    for dense in (left_dense, right_dense, later):
        dense[...] = jnp.zeros_like(dense)
    copy.wait()
    for step in range(EARLY):
        place(tiles[2 * step], table, 2 * step, left_dense, step * TILE, "left")
        place(tiles[2 * step + 1], table, 2 * step + 1, right_dense, step * TILE, "right")
    place(right_3, table, 2 * EARLY, later, 0, "right")
    for low in range(0, TILE, 2 * BLK):
        accum[:, low : low + 2 * BLK] = jnp.dot(
            left_dense[0:TILE, :],
            right_dense[0 : EARLY * TILE, low : low + 2 * BLK],
            preferred_element_type=jnp.float32,
        )


def late_kernel(on_diagonal, accum, right_dense, left_3, out, sums, left_dense, cells, table, sem):
    copy = gather_cells((left_3,), cells, table, sem)
    left_dense[...] = jnp.zeros_like(left_dense)
    copy.wait()
    place(left_3, table, 0, left_dense, 0, "left")
    width = 2 * BLK
    square_sum = jnp.float32(0)
    diagonal_sum = jnp.float32(0)
    inside = lax.broadcasted_iota(jnp.int32, (width, width), 0) == lax.broadcasted_iota(
        jnp.int32, (width, width), 1
    )
    for low in range(0, TILE, width):
        total = accum[:, low : low + width] + jnp.dot(
            left_dense[0:TILE, :],
            right_dense[0:TILE, low : low + width],
            preferred_element_type=jnp.float32,
        )
        out[:, low : low + width] = total.astype(out.dtype)
        square_sum += jnp.sum(total * total)
        diagonal_sum += jnp.sum(jnp.where(inside, total[low : low + width, :], 0.0))
    diagonal_sum = jnp.where(on_diagonal[0] > 0, diagonal_sum, 0.0)
    lane = lax.broadcasted_iota(jnp.int32, sums.shape, 1)
    sums[...] = jnp.where(lane == 0, diagonal_sum, jnp.where(lane == 1, square_sum, 0.0))


WHOLE = pl.BlockSpec(memory_space=pltpu.VMEM)
EARLY = STEPS - 1
CELLS = [pltpu.VMEM((8, LANES), jnp.int32), pltpu.SMEM((8, LANES), jnp.int32), pltpu.SemaphoreType.DMA]


def left_shape(steps):
    return (TILE + BLK, steps * TILE)


def right_shape(steps):
    return (steps * TILE + BLK, TILE)


def multiply_early(tiles):
    return pl.pallas_call(
        early_kernel,
        out_shape=(
            jax.ShapeDtypeStruct((TILE, TILE), jnp.float32),
            jax.ShapeDtypeStruct(right_shape(1), jnp.bfloat16),
        ),
        in_specs=[WHOLE] * len(tiles),
        out_specs=(WHOLE, WHOLE),
        scratch_shapes=[pltpu.VMEM(left_shape(EARLY), jnp.bfloat16), pltpu.VMEM(right_shape(EARLY), jnp.bfloat16)] + CELLS,
        compiler_params=pltpu.CompilerParams(vmem_limit_bytes=24 * 2**20),
        cost_estimate=pl.CostEstimate(flops=2 * EARLY * TILE**3, bytes_accessed=10_000_000, transcendentals=0),
        name="first_three_products",
    )(*tiles)


def multiply_late(on_diagonal, accum, right_dense, left_tile, fan):
    return pl.pallas_call(
        late_kernel,
        out_shape=(
            jax.ShapeDtypeStruct((TILE, TILE), jnp.bfloat16),
            jax.ShapeDtypeStruct((fan, LANES), jnp.float32),
        ),
        in_specs=[pl.BlockSpec(memory_space=pltpu.SMEM)] + [WHOLE] * 3,
        out_specs=(WHOLE, WHOLE),
        scratch_shapes=[pltpu.VMEM(left_shape(1), jnp.bfloat16)] + CELLS,
        compiler_params=pltpu.CompilerParams(vmem_limit_bytes=16 * 2**20),
        cost_estimate=pl.CostEstimate(flops=2 * TILE**3, bytes_accessed=6_000_000, transcendentals=0),
        name="last_product",
    )(on_diagonal, accum, right_dense, left_tile)


def exchange(value, target, rows, cols):
    pairs = []
    for i in range(rows):
        for j in range(cols):
            to_row, to_col = target(i, j)
            pairs.append((i * cols + j, to_row % rows * cols + to_col % cols))
    return lax.ppermute(value, BOTH, pairs)


def spread_sum(values, axis):
    return lax.all_to_all(values, axis, 0, 0, tiled=True)


def body(left_blocks, left_slots, right_blocks, right_slots):
    rows, cols = lax.axis_size("row"), lax.axis_size("col")
    on_diagonal = (lax.axis_index("row") == lax.axis_index("col")).astype(jnp.int32).reshape(1)
    left, right = pack(
        left_slots, right_slots, left_blocks.reshape(-1, LANES), right_blocks.reshape(-1, LANES)
    )
    move = functools.partial(exchange, rows=rows, cols=cols)
    left_first = move(left, lambda i, j: (i, j - 1 if i % 2 == 0 else j - 3))
    right_middle = move(right, lambda i, j: (i - 2, j))
    left_second = move(left, lambda i, j: (i, j - 3 if i % 2 == 0 else j - 1))
    right_first = move(right, lambda i, j: (i - 1 if i % 2 else i - 3, j))
    left_middle = move(left_first, lambda i, j: (i, j - 1 if i % 2 == 0 else j + 1))
    right_second = move(right_middle, lambda i, j: (i ^ 1, j))
    accum, later = multiply_early((left, right, left_first, right_first, left_second, right_second, right_middle))
    product, partial = multiply_late(on_diagonal, accum, later, left_middle, rows)
    row_sums = jnp.sum(spread_sum(partial, "row"), axis=0, keepdims=True)
    totals = jnp.sum(spread_sum(jnp.broadcast_to(row_sums, (cols, LANES)), "col"), axis=0)
    trace_scaled = totals[0] / math.sqrt(min(rows, cols) * TILE)
    norm_scaled = totals[1] / (rows * cols * TILE * TILE)
    return product, trace_scaled, norm_scaled


def solution(mesh):
    placed = (
        P("row", "col", None, None),
        P("row", "col"),
        P("row", "col", None, None),
        P("row", "col"),
    )
    return jax.shard_map(
        body, mesh=mesh, in_specs=placed, out_specs=(P("row", "col"), P(), P()), check_vma=False
    )
```

```python
import functools
import math

import jax
import jax.numpy as jnp
from jax import lax
from jax.experimental import pallas as pl
from jax.experimental.pallas import tpu as pltpu
from jax.sharding import PartitionSpec as P

BLK = 128
TB = 6
STEPS = 4
TILE = TB * BLK
WIDTH = 2 * BLK
TAIL = 16
LANES = 128
BOTH = ("row", "col")


def pack_kernel(left_slots, right_slots, left, right, left_out, right_out, held, read_sems, write_sems, tail_sems):
    depth = left.shape[0]
    part = depth // PARTS
    sides = ((right_slots, right, right_out), (left_slots, left, left_out))
    reads = []
    for side, (_, source, _) in enumerate(sides):
        for index in range(PARTS):
            rows = pl.ds(index * part, part)
            reads.append(pltpu.make_async_copy(source.at[rows], held.at[side, rows], read_sems.at[side, index]))
            reads[-1].start()
    lane = lax.broadcasted_iota(jnp.int32, (TAIL, LANES), 1)
    tail = pl.ds(depth, TAIL)
    writes = []
    for side, (slots, _, out) in enumerate(sides):
        cells = jnp.zeros((TAIL, LANES), jnp.int32)
        for slot in range(slots.shape[1]):
            cells = jnp.where(lane == slot, slots[0, slot], cells)
        held[side, depth : depth + TAIL, :] = cells.astype(jnp.float32).astype(out.dtype)
        writes.append(pltpu.make_async_copy(held.at[side, tail], out.at[tail], tail_sems.at[side]))
        writes[-1].start()
    for side, (_, _, out) in enumerate(sides):
        for index in range(PARTS):
            rows = pl.ds(index * part, part)
            reads[side * PARTS + index].wait()
            writes.append(pltpu.make_async_copy(held.at[side, rows], out.at[rows], write_sems.at[side, index]))
            writes[-1].start()
    for copy in writes:
        copy.wait()


PARTS = 3


def pack(left_slots, right_slots, left, right):
    depth = left.shape[0]
    packed = jax.ShapeDtypeStruct((depth + TAIL, LANES), left.dtype)
    return pl.pallas_call(
        pack_kernel,
        out_shape=(packed, packed),
        in_specs=[pl.BlockSpec(memory_space=pltpu.SMEM)] * 2 + [pl.BlockSpec(memory_space=pl.ANY)] * 2,
        out_specs=(pl.BlockSpec(memory_space=pl.ANY),) * 2,
        scratch_shapes=[
            pltpu.VMEM((2, depth + TAIL, LANES), left.dtype),
            pltpu.SemaphoreType.DMA((2, PARTS)),
            pltpu.SemaphoreType.DMA((2, PARTS)),
            pltpu.SemaphoreType.DMA((2,)),
        ],
        name="pack_tiles",
    )(left_slots, right_slots, left, right)


def gather_cells(tiles, cells, table, sem):
    depth = tiles[0].shape[0] - TAIL
    level = lax.broadcasted_iota(jnp.int32, cells.shape, 0)
    gathered = jnp.zeros(cells.shape, jnp.int32)
    for index, tile in enumerate(tiles):
        tail = tile[depth : depth + TAIL, :].astype(jnp.float32).astype(jnp.int32)
        gathered = jnp.where(level == index, tail[0 : cells.shape[0]], gathered)
    cells[...] = gathered
    copy = pltpu.make_async_copy(cells, table, sem)
    copy.start()
    return copy


def place(tile, table, index, dense, base, side):
    for slot in range((tile.shape[0] - TAIL) // BLK):
        cell = table[index, slot]
        row, col = cell // TB * BLK, cell % TB * BLK
        if side == "left":
            col = base + col
        else:
            row = jnp.where(cell < TB * TB, base + row, dense.shape[0] - BLK)
        row, col = pl.multiple_of(row, BLK), pl.multiple_of(col, BLK)
        dense[pl.ds(row, BLK), pl.ds(col, BLK)] = tile[slot * BLK : (slot + 1) * BLK, :]


def early_kernel(*refs):
    tiles, (accum, left_dense, right_dense, cells, table, sem) = refs[: 2 * EARLY], refs[2 * EARLY :]
    place_pairs(tiles, left_dense, right_dense, cells, table, sem)
    for low in range(0, TILE, WIDTH):
        accum[:, low : low + WIDTH] = multiply_pairs(left_dense, right_dense, low)


def late_kernel(on_diagonal, accum, *refs):
    tiles, rest = refs[: 2 * LATE], refs[2 * LATE :]
    out, sums, left_dense, right_dense, cells, table, sem, rounded, out_sems = rest
    place_pairs(tiles, left_dense, right_dense, cells, table, sem)
    inside = lax.broadcasted_iota(jnp.int32, (BLK, BLK), 0) == lax.broadcasted_iota(jnp.int32, (BLK, BLK), 1)
    squares = jnp.zeros((8, WIDTH), jnp.float32)
    diagonal = jnp.zeros((8, BLK), jnp.float32)
    copies = []
    for part in range(TILE // WIDTH):
        low = part * WIDTH
        columns = pl.ds(low, WIDTH)
        total = accum[:, low : low + WIDTH] + multiply_pairs(left_dense, right_dense, low)
        rounded[:, low : low + WIDTH] = total.astype(rounded.dtype)
        copies.append(pltpu.make_async_copy(rounded.at[:, columns], out.at[:, columns], out_sems.at[part]))
        copies[-1].start()
        squares += jnp.sum((total * total).reshape(-1, 8, WIDTH), axis=0)
        for block in range(0, WIDTH, BLK):
            corner = total[low + block : low + block + BLK, block : block + BLK]
            diagonal += jnp.sum(jnp.where(inside, corner, 0.0).reshape(-1, 8, BLK), axis=0)
    diagonal_sum = jnp.where(on_diagonal[0] > 0, jnp.sum(diagonal), 0.0)
    lane = lax.broadcasted_iota(jnp.int32, sums.shape, 1)
    sums[...] = jnp.where(lane == 0, diagonal_sum, jnp.where(lane == 1, jnp.sum(squares), 0.0))
    for copy in copies:
        copy.wait()


def place_pairs(tiles, left_dense, right_dense, cells, table, sem):
    copy = gather_cells(tiles, cells, table, sem)
    left_dense[...] = jnp.zeros_like(left_dense)
    right_dense[...] = jnp.zeros_like(right_dense)
    copy.wait()
    for step in range(len(tiles) // 2):
        place(tiles[2 * step], table, 2 * step, left_dense, step * TILE, "left")
        place(tiles[2 * step + 1], table, 2 * step + 1, right_dense, step * TILE, "right")


def multiply_pairs(left_dense, right_dense, low):
    depth = left_dense.shape[1]
    return jnp.dot(
        left_dense[0:TILE, :],
        right_dense[0:depth, low : low + WIDTH],
        preferred_element_type=jnp.float32,
    )


WHOLE = pl.BlockSpec(memory_space=pltpu.VMEM)
EARLY = 2
LATE = STEPS - EARLY
CELLS = [pltpu.VMEM((8, LANES), jnp.int32), pltpu.SMEM((8, LANES), jnp.int32), pltpu.SemaphoreType.DMA]


def left_shape(steps):
    return (TILE + BLK, steps * TILE)


def right_shape(steps):
    return (steps * TILE + BLK, TILE)


def scratch(steps):
    return [pltpu.VMEM(left_shape(steps), jnp.bfloat16), pltpu.VMEM(right_shape(steps), jnp.bfloat16)] + CELLS


def multiply_early(tiles):
    return pl.pallas_call(
        early_kernel,
        out_shape=jax.ShapeDtypeStruct((TILE, TILE), jnp.float32),
        in_specs=[WHOLE] * len(tiles),
        out_specs=WHOLE,
        scratch_shapes=scratch(EARLY),
        compiler_params=pltpu.CompilerParams(vmem_limit_bytes=24 * 2**20),
        cost_estimate=pl.CostEstimate(flops=2 * EARLY * TILE**3, bytes_accessed=5_000_000, transcendentals=0),
        name="early_products",
    )(*tiles)


def multiply_late(on_diagonal, accum, tiles, fan):
    return pl.pallas_call(
        late_kernel,
        out_shape=(
            jax.ShapeDtypeStruct((TILE, TILE), jnp.bfloat16),
            jax.ShapeDtypeStruct((fan, LANES), jnp.float32),
        ),
        in_specs=[pl.BlockSpec(memory_space=pltpu.SMEM)] + [WHOLE] * (1 + len(tiles)),
        out_specs=(pl.BlockSpec(memory_space=pl.ANY), WHOLE),
        scratch_shapes=scratch(LATE)
        + [pltpu.VMEM((TILE, TILE), jnp.bfloat16), pltpu.SemaphoreType.DMA((TILE // WIDTH,))],
        compiler_params=pltpu.CompilerParams(vmem_limit_bytes=24 * 2**20),
        cost_estimate=pl.CostEstimate(flops=2 * LATE * TILE**3, bytes_accessed=6_000_000, transcendentals=0),
        name="late_products",
    )(on_diagonal, accum, *tiles)


def exchange(value, target, rows, cols):
    pairs = []
    for i in range(rows):
        for j in range(cols):
            to_row, to_col = target(i, j)
            pairs.append((i * cols + j, to_row % rows * cols + to_col % cols))
    return lax.ppermute(value, BOTH, pairs)


def spread_sum(values, axis):
    return lax.all_to_all(values, axis, 0, 0, tiled=True)


def body(left_blocks, left_slots, right_blocks, right_slots):
    rows, cols = lax.axis_size("row"), lax.axis_size("col")
    on_diagonal = (lax.axis_index("row") == lax.axis_index("col")).astype(jnp.int32).reshape(1)
    left, right = pack(
        left_slots, right_slots, left_blocks.reshape(-1, LANES), right_blocks.reshape(-1, LANES)
    )
    move = functools.partial(exchange, rows=rows, cols=cols)
    left_first = move(left, lambda i, j: (i, j - 1 if i % 2 == 0 else j - 3))
    right_middle = move(right, lambda i, j: (i - 2, j))
    left_second = move(left, lambda i, j: (i, j - 3 if i % 2 == 0 else j - 1))
    right_first = move(right, lambda i, j: (i - 1 if i % 2 else i - 3, j))
    left_middle = move(left_first, lambda i, j: (i, j - 1 if i % 2 == 0 else j + 1))
    right_second = move(right_middle, lambda i, j: (i ^ 1, j))
    accum = multiply_early((left, right, left_first, right_first))
    late = (left_middle, right_middle, left_second, right_second)
    product, partial = multiply_late(on_diagonal, accum, late, rows)
    row_sums = jnp.sum(spread_sum(partial, "row"), axis=0, keepdims=True)
    totals = jnp.sum(spread_sum(jnp.broadcast_to(row_sums, (cols, LANES)), "col"), axis=0)
    trace_scaled = totals[0] / math.sqrt(min(rows, cols) * TILE)
    norm_scaled = totals[1] / (rows * cols * TILE * TILE)
    return product, trace_scaled, norm_scaled


def solution(mesh):
    placed = (
        P("row", "col", None, None),
        P("row", "col"),
        P("row", "col", None, None),
        P("row", "col"),
    )
    return jax.shard_map(
        body, mesh=mesh, in_specs=placed, out_specs=(P("row", "col"), P(), P()), check_vma=False
    )
```

```python
import functools
import math

import jax
import jax.numpy as jnp
from jax import lax
from jax.experimental import pallas as pl
from jax.experimental.pallas import tpu as pltpu
from jax.sharding import PartitionSpec as P

BLK = 128
TB = 6
STEPS = 4
TILE = TB * BLK
WIDTH = 2 * BLK
TAIL = 16
LANES = 128
BOTH = ("row", "col")


def pack_kernel(left_slots, right_slots, left, right, left_out, right_out, held, table, read_sems, write_sems, tail_sems, slot_sems):
    depth = left.shape[0]
    part = depth // PARTS
    sides = ((left_slots, left, left_out), (right_slots, right, right_out))
    fetches = []
    for side, (slots, _, _) in enumerate(sides):
        fetches.append(pltpu.make_async_copy(slots, table.at[side], slot_sems.at[side]))
        fetches[-1].start()
    reads = []
    for side, (_, source, _) in enumerate(sides):
        for index in range(PARTS):
            rows = pl.ds(index * part, part)
            reads.append(pltpu.make_async_copy(source.at[rows], held.at[side, rows], read_sems.at[side, index]))
            reads[-1].start()
    lane = lax.broadcasted_iota(jnp.int32, (TAIL, LANES), 1)
    tail = pl.ds(depth, TAIL)
    writes = []
    for side, (slots, _, out) in enumerate(sides):
        fetches[side].wait()
        cells = jnp.zeros((TAIL, LANES), jnp.int32)
        for slot in range(slots.shape[1]):
            cells = jnp.where(lane == slot, table[side, 0, slot], cells)
        held[side, depth : depth + TAIL, :] = cells.astype(jnp.float32).astype(out.dtype)
        writes.append(pltpu.make_async_copy(held.at[side, tail], out.at[tail], tail_sems.at[side]))
        writes[-1].start()
    for side, (_, _, out) in enumerate(sides):
        for index in range(PARTS):
            rows = pl.ds(index * part, part)
            reads[side * PARTS + index].wait()
            writes.append(pltpu.make_async_copy(held.at[side, rows], out.at[rows], write_sems.at[side, index]))
            writes[-1].start()
    for copy in writes:
        copy.wait()


PARTS = 3


def pack(left_slots, right_slots, left, right):
    depth = left.shape[0]
    packed = jax.ShapeDtypeStruct((depth + TAIL, LANES), left.dtype)
    return pl.pallas_call(
        pack_kernel,
        out_shape=(packed, packed),
        in_specs=[pl.BlockSpec(memory_space=pl.ANY)] * 4,
        out_specs=(pl.BlockSpec(memory_space=pl.ANY),) * 2,
        scratch_shapes=[
            pltpu.VMEM((2, depth + TAIL, LANES), left.dtype),
            pltpu.SMEM((2,) + left_slots.shape, jnp.int32),
            pltpu.SemaphoreType.DMA((2, PARTS)),
            pltpu.SemaphoreType.DMA((2, PARTS)),
            pltpu.SemaphoreType.DMA((2,)),
            pltpu.SemaphoreType.DMA((2,)),
        ],
        name="pack_tiles",
    )(left_slots, right_slots, left, right)


def gather_cells(tiles, cells, table, sem):
    depth = tiles[0].shape[0] - TAIL
    level = lax.broadcasted_iota(jnp.int32, cells.shape, 0)
    gathered = jnp.zeros(cells.shape, jnp.int32)
    for index, tile in enumerate(tiles):
        tail = tile[depth : depth + TAIL, :].astype(jnp.float32).astype(jnp.int32)
        gathered = jnp.where(level == index, tail[0 : cells.shape[0]], gathered)
    cells[...] = gathered
    copy = pltpu.make_async_copy(cells, table, sem)
    copy.start()
    return copy


def place(tile, table, index, dense, base, side):
    for slot in range((tile.shape[0] - TAIL) // BLK):
        cell = table[index, slot]
        row, col = cell // TB * BLK, cell % TB * BLK
        if side == "left":
            col = base + col
        else:
            row = jnp.where(cell < TB * TB, base + row, dense.shape[0] - BLK)
        row, col = pl.multiple_of(row, BLK), pl.multiple_of(col, BLK)
        dense[pl.ds(row, BLK), pl.ds(col, BLK)] = tile[slot * BLK : (slot + 1) * BLK, :]


def first_kernel(left_0, right_0, left_1, right_1, accum, *scratches):
    left_dense, right_dense, cells, table, sem = scratches
    place_pairs((left_0, right_0, left_1, right_1), left_dense, right_dense, cells, table, sem)
    for low in range(0, TILE, WIDTH):
        accum[:, low : low + WIDTH] = multiply_pairs(left_dense, right_dense, low)


def next_kernel(before, left_2, right_2, accum, *scratches):
    left_dense, right_dense, cells, table, sem = scratches
    place_pairs((left_2, right_2), left_dense, right_dense, cells, table, sem)
    for low in range(0, TILE, WIDTH):
        accum[:, low : low + WIDTH] = before[:, low : low + WIDTH] + multiply_pairs(left_dense, right_dense, low)


def last_kernel(on_diagonal, accum, *refs):
    out, sums, left_dense, right_dense, cells, table, sem, rounded, out_sems = refs[-9:]
    place_pairs(refs[:-9], left_dense, right_dense, cells, table, sem)
    inside = lax.broadcasted_iota(jnp.int32, (BLK, BLK), 0) == lax.broadcasted_iota(jnp.int32, (BLK, BLK), 1)
    squares = jnp.zeros((8, WIDTH), jnp.float32)
    diagonal = jnp.zeros((8, BLK), jnp.float32)
    copies = []
    for part in range(TILE // WIDTH):
        low = part * WIDTH
        columns = pl.ds(low, WIDTH)
        total = accum[:, low : low + WIDTH] + multiply_pairs(left_dense, right_dense, low)
        rounded[:, low : low + WIDTH] = total.astype(rounded.dtype)
        copies.append(pltpu.make_async_copy(rounded.at[:, columns], out.at[:, columns], out_sems.at[part]))
        copies[-1].start()
        squares += jnp.sum((total * total).reshape(-1, 8, WIDTH), axis=0)
        for block in range(0, WIDTH, BLK):
            corner = total[low + block : low + block + BLK, block : block + BLK]
            diagonal += jnp.sum(jnp.where(inside, corner, 0.0).reshape(-1, 8, BLK), axis=0)
    diagonal_sum = jnp.where(on_diagonal[0] > 0, jnp.sum(diagonal), 0.0)
    lane = lax.broadcasted_iota(jnp.int32, sums.shape, 1)
    sums[...] = jnp.where(lane == 0, diagonal_sum, jnp.where(lane == 1, jnp.sum(squares), 0.0))
    for copy in copies:
        copy.wait()


def place_pairs(tiles, left_dense, right_dense, cells, table, sem):
    copy = gather_cells(tiles, cells, table, sem)
    left_dense[...] = jnp.zeros_like(left_dense)
    right_dense[...] = jnp.zeros_like(right_dense)
    copy.wait()
    for step in range(len(tiles) // 2):
        place(tiles[2 * step], table, 2 * step, left_dense, step * TILE, "left")
        place(tiles[2 * step + 1], table, 2 * step + 1, right_dense, step * TILE, "right")


def multiply_pairs(left_dense, right_dense, low):
    depth = left_dense.shape[1]
    return jnp.dot(
        left_dense[0:TILE, :],
        right_dense[0:depth, low : low + WIDTH],
        preferred_element_type=jnp.float32,
    )


WHOLE = pl.BlockSpec(memory_space=pltpu.VMEM)
CELLS = [pltpu.VMEM((8, LANES), jnp.int32), pltpu.SMEM((8, LANES), jnp.int32), pltpu.SemaphoreType.DMA]


def left_shape(steps):
    return (TILE + BLK, steps * TILE)


def right_shape(steps):
    return (steps * TILE + BLK, TILE)


def scratch(steps):
    return [pltpu.VMEM(left_shape(steps), jnp.bfloat16), pltpu.VMEM(right_shape(steps), jnp.bfloat16)] + CELLS


LIMIT = pltpu.CompilerParams(vmem_limit_bytes=20 * 2**20)
SMALL = pl.CostEstimate(flops=1000, bytes_accessed=1000, transcendentals=0)


def multiply(kernel, name, inputs, steps):
    return pl.pallas_call(
        kernel,
        out_shape=jax.ShapeDtypeStruct((TILE, TILE), jnp.float32),
        in_specs=[WHOLE] * len(inputs),
        out_specs=WHOLE,
        scratch_shapes=scratch(steps),
        compiler_params=LIMIT,
        cost_estimate=SMALL,
        name=name,
    )(*inputs)


def multiply_last(on_diagonal, inputs, fan):
    return pl.pallas_call(
        last_kernel,
        out_shape=(
            jax.ShapeDtypeStruct((TILE, TILE), jnp.bfloat16),
            jax.ShapeDtypeStruct((fan, LANES), jnp.float32),
        ),
        in_specs=[pl.BlockSpec(memory_space=pltpu.SMEM)] + [WHOLE] * len(inputs),
        out_specs=(pl.BlockSpec(memory_space=pl.ANY), WHOLE),
        scratch_shapes=scratch((len(inputs) - 1) // 2)
        + [pltpu.VMEM((TILE, TILE), jnp.bfloat16), pltpu.SemaphoreType.DMA((TILE // WIDTH,))],
        compiler_params=LIMIT,
        cost_estimate=SMALL,
        name="last_product",
    )(on_diagonal, *inputs)


def exchange(value, target, rows, cols):
    pairs = []
    for i in range(rows):
        for j in range(cols):
            to_row, to_col = target(i, j)
            pairs.append((i * cols + j, to_row % rows * cols + to_col % cols))
    return lax.ppermute(value, BOTH, pairs)


def spread_sum(values, axis):
    return lax.all_to_all(values, axis, 0, 0, tiled=True)


def body(left_blocks, left_slots, right_blocks, right_slots):
    rows, cols = lax.axis_size("row"), lax.axis_size("col")
    on_diagonal = (lax.axis_index("row") == lax.axis_index("col")).astype(jnp.int32).reshape(1)
    left, right = pack(
        left_slots, right_slots, left_blocks.reshape(-1, LANES), right_blocks.reshape(-1, LANES)
    )
    move = functools.partial(exchange, rows=rows, cols=cols)
    left_first = move(left, lambda i, j: (i, j - 1 if i % 2 == 0 else j - 3))
    right_middle = move(right, lambda i, j: (i - 2, j))
    left_second = move(left, lambda i, j: (i, j - 3 if i % 2 == 0 else j - 1))
    right_first = move(right, lambda i, j: (i - 1 if i % 2 else i - 3, j))
    left_middle = move(left_first, lambda i, j: (i, j - 1 if i % 2 == 0 else j + 1))
    right_second = move(right_middle, lambda i, j: (i ^ 1, j))
    accum = multiply(first_kernel, "first_products", (left, right, left_first, right_first), 2)
    accum = multiply(next_kernel, "next_product", (accum, left_middle, right_middle), 1)
    product, partial = multiply_last(on_diagonal, (accum, left_second, right_second), rows)
    row_sums = jnp.sum(spread_sum(partial, "row"), axis=0, keepdims=True)
    totals = jnp.sum(spread_sum(jnp.broadcast_to(row_sums, (cols, LANES)), "col"), axis=0)
    trace_scaled = totals[0] / math.sqrt(min(rows, cols) * TILE)
    norm_scaled = totals[1] / (rows * cols * TILE * TILE)
    return product, trace_scaled, norm_scaled


def solution(mesh):
    placed = (
        P("row", "col", None, None),
        P("row", "col"),
        P("row", "col", None, None),
        P("row", "col"),
    )
    return jax.shard_map(
        body, mesh=mesh, in_specs=placed, out_specs=(P("row", "col"), P(), P()), check_vma=False
    )
```

```python
import functools
import math

import jax
import jax.numpy as jnp
from jax import lax
from jax.experimental import pallas as pl
from jax.experimental.pallas import tpu as pltpu
from jax.sharding import PartitionSpec as P

BLK = 128
TB = 6
STEPS = 4
TILE = TB * BLK
WIDTH = 2 * BLK
TAIL = 16
LANES = 128
BOTH = ("row", "col")


def pack_kernel(left_slots, right_slots, left, right, left_out, right_out, held, table, read_sems, write_sems, tail_sems, slot_sems):
    depth = left.shape[0]
    part = depth // PARTS
    sides = ((left_slots, left, left_out), (right_slots, right, right_out))
    fetches = []
    for side, (slots, _, _) in enumerate(sides):
        fetches.append(pltpu.make_async_copy(slots, table.at[side], slot_sems.at[side]))
        fetches[-1].start()
    reads = []
    for side, (_, source, _) in enumerate(sides):
        for index in range(PARTS):
            rows = pl.ds(index * part, part)
            reads.append(pltpu.make_async_copy(source.at[rows], held.at[side, rows], read_sems.at[side, index]))
            reads[-1].start()
    lane = lax.broadcasted_iota(jnp.int32, (TAIL, LANES), 1)
    tail = pl.ds(depth, TAIL)
    writes = []
    for side, (slots, _, out) in enumerate(sides):
        fetches[side].wait()
        cells = jnp.zeros((TAIL, LANES), jnp.int32)
        for slot in range(slots.shape[1]):
            cells = jnp.where(lane == slot, table[side, 0, slot], cells)
        held[side, depth : depth + TAIL, :] = cells.astype(jnp.float32).astype(out.dtype)
        writes.append(pltpu.make_async_copy(held.at[side, tail], out.at[tail], tail_sems.at[side]))
        writes[-1].start()
    for side, (_, _, out) in enumerate(sides):
        for index in range(PARTS):
            rows = pl.ds(index * part, part)
            reads[side * PARTS + index].wait()
            writes.append(pltpu.make_async_copy(held.at[side, rows], out.at[rows], write_sems.at[side, index]))
            writes[-1].start()
    for copy in writes:
        copy.wait()


PARTS = 3


def pack(left_slots, right_slots, left, right):
    depth = left.shape[0]
    packed = jax.ShapeDtypeStruct((depth + TAIL, LANES), left.dtype)
    return pl.pallas_call(
        pack_kernel,
        out_shape=(packed, packed),
        in_specs=[pl.BlockSpec(memory_space=pl.ANY)] * 4,
        out_specs=(pl.BlockSpec(memory_space=pl.ANY),) * 2,
        scratch_shapes=[
            pltpu.VMEM((2, depth + TAIL, LANES), left.dtype),
            pltpu.SMEM((2,) + left_slots.shape, jnp.int32),
            pltpu.SemaphoreType.DMA((2, PARTS)),
            pltpu.SemaphoreType.DMA((2, PARTS)),
            pltpu.SemaphoreType.DMA((2,)),
            pltpu.SemaphoreType.DMA((2,)),
        ],
        name="pack_tiles",
    )(left_slots, right_slots, left, right)


def gather_cells(tiles, cells, table, sem):
    depth = tiles[0].shape[0] - TAIL
    level = lax.broadcasted_iota(jnp.int32, cells.shape, 0)
    gathered = jnp.zeros(cells.shape, jnp.int32)
    for index, tile in enumerate(tiles):
        tail = tile[depth : depth + TAIL, :].astype(jnp.float32).astype(jnp.int32)
        gathered = jnp.where(level == index, tail[0 : cells.shape[0]], gathered)
    cells[...] = gathered
    copy = pltpu.make_async_copy(cells, table, sem)
    copy.start()
    return copy


def place(tile, table, index, dense, base, side):
    for slot in range((tile.shape[0] - TAIL) // BLK):
        cell = table[index, slot]
        row, col = cell // TB * BLK, cell % TB * BLK
        if side == "left":
            col = base + col
        else:
            row = jnp.where(cell < TB * TB, base + row, dense.shape[0] - BLK)
        row, col = pl.multiple_of(row, BLK), pl.multiple_of(col, BLK)
        dense[pl.ds(row, BLK), pl.ds(col, BLK)] = tile[slot * BLK : (slot + 1) * BLK, :]


def first_kernel(left_0, right_0, left_1, right_1, accum, *scratches):
    left_dense, right_dense, cells, table, sem = scratches
    place_pairs((left_0, right_0, left_1, right_1), left_dense, right_dense, cells, table, sem)
    for low in range(0, TILE, WIDTH):
        accum[:, low : low + WIDTH] = multiply_pairs(left_dense, right_dense, low)


def next_kernel(before, left_2, right_2, accum, *scratches):
    left_dense, right_dense, cells, table, sem = scratches
    place_pairs((left_2, right_2), left_dense, right_dense, cells, table, sem)
    for low in range(0, TILE, WIDTH):
        accum[:, low : low + WIDTH] = before[:, low : low + WIDTH] + multiply_pairs(left_dense, right_dense, low)


def last_kernel(on_diagonal, accum, *refs):
    out, sums, left_dense, right_dense, cells, table, sem, rounded, out_sems = refs[-9:]
    place_pairs(refs[:-9], left_dense, right_dense, cells, table, sem)
    inside = lax.broadcasted_iota(jnp.int32, (BLK, BLK), 0) == lax.broadcasted_iota(jnp.int32, (BLK, BLK), 1)
    squares = jnp.zeros((8, WIDTH), jnp.float32)
    diagonal = jnp.zeros((8, BLK), jnp.float32)
    copies = []
    for part in range(TILE // WIDTH):
        low = part * WIDTH
        columns = pl.ds(low, WIDTH)
        total = accum[:, low : low + WIDTH] + multiply_pairs(left_dense, right_dense, low)
        rounded[:, low : low + WIDTH] = total.astype(rounded.dtype)
        copies.append(pltpu.make_async_copy(rounded.at[:, columns], out.at[:, columns], out_sems.at[part]))
        copies[-1].start()
        squares += jnp.sum((total * total).reshape(-1, 8, WIDTH), axis=0)
        for block in range(0, WIDTH, BLK):
            corner = total[low + block : low + block + BLK, block : block + BLK]
            diagonal += jnp.sum(jnp.where(inside, corner, 0.0).reshape(-1, 8, BLK), axis=0)
    diagonal_sum = jnp.where(on_diagonal[0] > 0, jnp.sum(diagonal), 0.0)
    lane = lax.broadcasted_iota(jnp.int32, sums.shape, 1)
    sums[...] = jnp.where(lane == 0, diagonal_sum, jnp.where(lane == 1, jnp.sum(squares), 0.0))
    for copy in copies:
        copy.wait()


def place_pairs(tiles, left_dense, right_dense, cells, table, sem):
    copy = gather_cells(tiles, cells, table, sem)
    left_dense[...] = jnp.zeros_like(left_dense)
    right_dense[...] = jnp.zeros_like(right_dense)
    copy.wait()
    for step in range(len(tiles) // 2):
        place(tiles[2 * step], table, 2 * step, left_dense, step * TILE, "left")
        place(tiles[2 * step + 1], table, 2 * step + 1, right_dense, step * TILE, "right")


def multiply_pairs(left_dense, right_dense, low):
    depth = left_dense.shape[1]
    return jnp.dot(
        left_dense[0:TILE, :],
        right_dense[0:depth, low : low + WIDTH],
        preferred_element_type=jnp.float32,
    )


WHOLE = pl.BlockSpec(memory_space=pltpu.VMEM)
CELLS = [pltpu.VMEM((8, LANES), jnp.int32), pltpu.SMEM((8, LANES), jnp.int32), pltpu.SemaphoreType.DMA]


def left_shape(steps):
    return (TILE + BLK, steps * TILE)


def right_shape(steps):
    return (steps * TILE + BLK, TILE)


def scratch(steps):
    return [pltpu.VMEM(left_shape(steps), jnp.bfloat16), pltpu.VMEM(right_shape(steps), jnp.bfloat16)] + CELLS


LIMIT = pltpu.CompilerParams(vmem_limit_bytes=20 * 2**20)
SMALL = pl.CostEstimate(flops=1000, bytes_accessed=1000, transcendentals=0)


def multiply(kernel, name, inputs, steps):
    return pl.pallas_call(
        kernel,
        out_shape=jax.ShapeDtypeStruct((TILE, TILE), jnp.float32),
        in_specs=[WHOLE] * len(inputs),
        out_specs=WHOLE,
        scratch_shapes=scratch(steps),
        compiler_params=LIMIT,
        cost_estimate=SMALL,
        name=name,
    )(*inputs)


def multiply_last(on_diagonal, inputs, fan):
    return pl.pallas_call(
        last_kernel,
        out_shape=(
            jax.ShapeDtypeStruct((TILE, TILE), jnp.bfloat16),
            jax.ShapeDtypeStruct((fan, LANES), jnp.float32),
        ),
        in_specs=[pl.BlockSpec(memory_space=pltpu.SMEM)] + [WHOLE] * len(inputs),
        out_specs=(pl.BlockSpec(memory_space=pl.ANY), WHOLE),
        scratch_shapes=scratch((len(inputs) - 1) // 2)
        + [pltpu.VMEM((TILE, TILE), jnp.bfloat16), pltpu.SemaphoreType.DMA((TILE // WIDTH,))],
        compiler_params=LIMIT,
        cost_estimate=SMALL,
        name="last_product",
    )(on_diagonal, *inputs)


def exchange(value, target, rows, cols):
    pairs = []
    for i in range(rows):
        for j in range(cols):
            to_row, to_col = target(i, j)
            pairs.append((i * cols + j, to_row % rows * cols + to_col % cols))
    return lax.ppermute(value, BOTH, pairs)


def spread_sum(values, axis):
    return lax.all_to_all(values, axis, 0, 0, tiled=True)


def body(left_blocks, left_slots, right_blocks, right_slots):
    rows, cols = lax.axis_size("row"), lax.axis_size("col")
    on_diagonal = (lax.axis_index("row") == lax.axis_index("col")).astype(jnp.int32).reshape(1)
    left, right = pack(
        left_slots, right_slots, left_blocks.reshape(-1, LANES), right_blocks.reshape(-1, LANES)
    )
    move = functools.partial(exchange, rows=rows, cols=cols)
    right_middle = move(right, lambda i, j: (i - 2, j))
    right_first = move(right, lambda i, j: (i - 1 if i % 2 else i - 3, j))
    left, right_first = lax.optimization_barrier((left, right_first))
    left_first = move(left, lambda i, j: (i, j - 1 if i % 2 == 0 else j - 3))
    left_second = move(left, lambda i, j: (i, j - 3 if i % 2 == 0 else j - 1))
    left_middle = move(left_first, lambda i, j: (i, j - 1 if i % 2 == 0 else j + 1))
    right_second = move(right_middle, lambda i, j: (i ^ 1, j))
    accum = multiply(first_kernel, "first_products", (left, right, left_first, right_first), 2)
    accum = multiply(next_kernel, "next_product", (accum, left_second, right_second), 1)
    product, partial = multiply_last(on_diagonal, (accum, left_middle, right_middle), rows)
    row_sums = jnp.sum(spread_sum(partial, "row"), axis=0, keepdims=True)
    totals = jnp.sum(spread_sum(jnp.broadcast_to(row_sums, (cols, LANES)), "col"), axis=0)
    trace_scaled = totals[0] / math.sqrt(min(rows, cols) * TILE)
    norm_scaled = totals[1] / (rows * cols * TILE * TILE)
    return product, trace_scaled, norm_scaled


def solution(mesh):
    placed = (
        P("row", "col", None, None),
        P("row", "col"),
        P("row", "col", None, None),
        P("row", "col"),
    )
    return jax.shard_map(
        body, mesh=mesh, in_specs=placed, out_specs=(P("row", "col"), P(), P()), check_vma=False
    )
```

```python
import functools
import math

import jax
import jax.numpy as jnp
from jax import lax
from jax.experimental import pallas as pl
from jax.experimental.pallas import tpu as pltpu
from jax.sharding import PartitionSpec as P

BLK = 128
TB = 6
STEPS = 4
TILE = TB * BLK
WIDTH = 2 * BLK
TAIL = 16
LANES = 128
BOTH = ("row", "col")


def pack_kernel(left_slots, right_slots, left, right, left_out, right_out, held, table, read_sems, write_sems, tail_sems, slot_sems):
    depth = left.shape[0]
    part = depth // PARTS
    sides = ((left_slots, left, left_out), (right_slots, right, right_out))
    fetches = []
    for side, (slots, _, _) in enumerate(sides):
        fetches.append(pltpu.make_async_copy(slots, table.at[side], slot_sems.at[side]))
        fetches[-1].start()
    reads = []
    for side, (_, source, _) in enumerate(sides):
        for index in range(PARTS):
            rows = pl.ds(index * part, part)
            reads.append(pltpu.make_async_copy(source.at[rows], held.at[side, rows], read_sems.at[side, index]))
            reads[-1].start()
    lane = lax.broadcasted_iota(jnp.int32, (TAIL, LANES), 1)
    tail = pl.ds(depth, TAIL)
    writes = []
    for side, (slots, _, out) in enumerate(sides):
        fetches[side].wait()
        cells = jnp.zeros((TAIL, LANES), jnp.int32)
        for slot in range(slots.shape[1]):
            cells = jnp.where(lane == slot, table[side, 0, slot], cells)
        held[side, depth : depth + TAIL, :] = cells.astype(jnp.float32).astype(out.dtype)
        writes.append(pltpu.make_async_copy(held.at[side, tail], out.at[tail], tail_sems.at[side]))
        writes[-1].start()
    for side, (_, _, out) in enumerate(sides):
        for index in range(PARTS):
            rows = pl.ds(index * part, part)
            reads[side * PARTS + index].wait()
            writes.append(pltpu.make_async_copy(held.at[side, rows], out.at[rows], write_sems.at[side, index]))
            writes[-1].start()
    for copy in writes:
        copy.wait()


PARTS = 3


def pack(left_slots, right_slots, left, right):
    depth = left.shape[0]
    packed = jax.ShapeDtypeStruct((depth + TAIL, LANES), left.dtype)
    return pl.pallas_call(
        pack_kernel,
        out_shape=(packed, packed),
        in_specs=[pl.BlockSpec(memory_space=pl.ANY)] * 4,
        out_specs=(pl.BlockSpec(memory_space=pl.ANY),) * 2,
        scratch_shapes=[
            pltpu.VMEM((2, depth + TAIL, LANES), left.dtype),
            pltpu.SMEM((2,) + left_slots.shape, jnp.int32),
            pltpu.SemaphoreType.DMA((2, PARTS)),
            pltpu.SemaphoreType.DMA((2, PARTS)),
            pltpu.SemaphoreType.DMA((2,)),
            pltpu.SemaphoreType.DMA((2,)),
        ],
        name="pack_tiles",
    )(left_slots, right_slots, left, right)


def gather_cells(tiles, cells, table, sem):
    depth = tiles[0].shape[0] - TAIL
    level = lax.broadcasted_iota(jnp.int32, cells.shape, 0)
    gathered = jnp.zeros(cells.shape, jnp.int32)
    for index, tile in enumerate(tiles):
        tail = tile[depth : depth + TAIL, :].astype(jnp.float32).astype(jnp.int32)
        gathered = jnp.where(level == index, tail[0 : cells.shape[0]], gathered)
    cells[...] = gathered
    copy = pltpu.make_async_copy(cells, table, sem)
    copy.start()
    return copy


def place(tile, table, index, dense, base, side):
    for slot in range((tile.shape[0] - TAIL) // BLK):
        cell = table[index, slot]
        row, col = cell // TB * BLK, cell % TB * BLK
        if side == "left":
            col = base + col
        else:
            row = jnp.where(cell < TB * TB, base + row, dense.shape[0] - BLK)
        row, col = pl.multiple_of(row, BLK), pl.multiple_of(col, BLK)
        dense[pl.ds(row, BLK), pl.ds(col, BLK)] = tile[slot * BLK : (slot + 1) * BLK, :]


def first_kernel(left_0, right_0, left_1, right_1, accum, *scratches):
    left_dense, right_dense, cells, table, sem = scratches
    place_pairs((left_0, right_0, left_1, right_1), left_dense, right_dense, cells, table, sem)
    for low in range(0, TILE, WIDTH):
        accum[:, low : low + WIDTH] = multiply_pairs(left_dense, right_dense, low)


def next_kernel(before, left_2, right_2, accum, *scratches):
    left_dense, right_dense, cells, table, sem = scratches
    place_pairs((left_2, right_2), left_dense, right_dense, cells, table, sem)
    for low in range(0, TILE, WIDTH):
        accum[:, low : low + WIDTH] = before[:, low : low + WIDTH] + multiply_pairs(left_dense, right_dense, low)


def last_kernel(on_diagonal, accum, left_3, right_3, out, sums, *scratches):
    left_dense, right_dense, cells, table, sem = scratches
    place_pairs((left_3, right_3), left_dense, right_dense, cells, table, sem)
    square_sum = jnp.float32(0)
    diagonal_sum = jnp.float32(0)
    inside = lax.broadcasted_iota(jnp.int32, (WIDTH, WIDTH), 0) == lax.broadcasted_iota(
        jnp.int32, (WIDTH, WIDTH), 1
    )
    for low in range(0, TILE, WIDTH):
        total = accum[:, low : low + WIDTH] + multiply_pairs(left_dense, right_dense, low)
        out[:, low : low + WIDTH] = total.astype(out.dtype)
        square_sum += jnp.sum(total * total)
        diagonal_sum += jnp.sum(jnp.where(inside, total[low : low + WIDTH, :], 0.0))
    diagonal_sum = jnp.where(on_diagonal[0] > 0, diagonal_sum, 0.0)
    lane = lax.broadcasted_iota(jnp.int32, sums.shape, 1)
    sums[...] = jnp.where(lane == 0, diagonal_sum, jnp.where(lane == 1, square_sum, 0.0))


def place_pairs(tiles, left_dense, right_dense, cells, table, sem):
    copy = gather_cells(tiles, cells, table, sem)
    left_dense[...] = jnp.zeros_like(left_dense)
    right_dense[...] = jnp.zeros_like(right_dense)
    copy.wait()
    for step in range(len(tiles) // 2):
        place(tiles[2 * step], table, 2 * step, left_dense, step * TILE, "left")
        place(tiles[2 * step + 1], table, 2 * step + 1, right_dense, step * TILE, "right")


def multiply_pairs(left_dense, right_dense, low):
    depth = left_dense.shape[1]
    return jnp.dot(
        left_dense[0:TILE, :],
        right_dense[0:depth, low : low + WIDTH],
        preferred_element_type=jnp.float32,
    )


WHOLE = pl.BlockSpec(memory_space=pltpu.VMEM)
CELLS = [pltpu.VMEM((8, LANES), jnp.int32), pltpu.SMEM((8, LANES), jnp.int32), pltpu.SemaphoreType.DMA]


def left_shape(steps):
    return (TILE + BLK, steps * TILE)


def right_shape(steps):
    return (steps * TILE + BLK, TILE)


def scratch(steps):
    return [pltpu.VMEM(left_shape(steps), jnp.bfloat16), pltpu.VMEM(right_shape(steps), jnp.bfloat16)] + CELLS


LIMIT = pltpu.CompilerParams(vmem_limit_bytes=20 * 2**20)
SMALL = pl.CostEstimate(flops=1000, bytes_accessed=1000, transcendentals=0)


def multiply(kernel, name, inputs, steps):
    return pl.pallas_call(
        kernel,
        out_shape=jax.ShapeDtypeStruct((TILE, TILE), jnp.float32),
        in_specs=[WHOLE] * len(inputs),
        out_specs=WHOLE,
        scratch_shapes=scratch(steps),
        compiler_params=LIMIT,
        cost_estimate=SMALL,
        name=name,
    )(*inputs)


def multiply_last(on_diagonal, inputs, fan):
    return pl.pallas_call(
        last_kernel,
        out_shape=(
            jax.ShapeDtypeStruct((TILE, TILE), jnp.bfloat16),
            jax.ShapeDtypeStruct((fan, LANES), jnp.float32),
        ),
        in_specs=[pl.BlockSpec(memory_space=pltpu.SMEM)] + [WHOLE] * len(inputs),
        out_specs=(WHOLE, WHOLE),
        scratch_shapes=scratch(1),
        compiler_params=LIMIT,
        cost_estimate=SMALL,
        name="last_product",
    )(on_diagonal, *inputs)


def exchange(value, target, rows, cols):
    pairs = []
    for i in range(rows):
        for j in range(cols):
            to_row, to_col = target(i, j)
            pairs.append((i * cols + j, to_row % rows * cols + to_col % cols))
    return lax.ppermute(value, BOTH, pairs)


def spread_sum(values, axis):
    return lax.all_to_all(values, axis, 0, 0, tiled=True)


def body(left_blocks, left_slots, right_blocks, right_slots):
    rows, cols = lax.axis_size("row"), lax.axis_size("col")
    on_diagonal = (lax.axis_index("row") == lax.axis_index("col")).astype(jnp.int32).reshape(1)
    left, right = pack(
        left_slots, right_slots, left_blocks.reshape(-1, LANES), right_blocks.reshape(-1, LANES)
    )
    move = functools.partial(exchange, rows=rows, cols=cols)
    left_first = move(left, lambda i, j: (i, j - 1 if i % 2 == 0 else j - 3))
    left_second = move(left, lambda i, j: (i, j - 3 if i % 2 == 0 else j - 1))
    left_middle = move(left_first, lambda i, j: (i, j - 1 if i % 2 == 0 else j + 1))
    right_first = move(right, lambda i, j: (i - 1 if i % 2 else i - 3, j))
    right_middle = move(right, lambda i, j: (i - 2, j))
    accum = multiply(first_kernel, "first_products", (left, right, left_first, right_first), 2)
    right_middle, accum = lax.optimization_barrier((right_middle, accum))
    right_second = move(right_middle, lambda i, j: (i ^ 1, j))
    accum = multiply(next_kernel, "next_product", (accum, left_middle, right_middle), 1)
    product, partial = multiply_last(on_diagonal, (accum, left_second, right_second), rows)
    row_sums = jnp.sum(spread_sum(partial, "row"), axis=0, keepdims=True)
    totals = jnp.sum(spread_sum(jnp.broadcast_to(row_sums, (cols, LANES)), "col"), axis=0)
    trace_scaled = totals[0] / math.sqrt(min(rows, cols) * TILE)
    norm_scaled = totals[1] / (rows * cols * TILE * TILE)
    return product, trace_scaled, norm_scaled


def solution(mesh):
    placed = (
        P("row", "col", None, None),
        P("row", "col"),
        P("row", "col", None, None),
        P("row", "col"),
    )
    return jax.shard_map(
        body, mesh=mesh, in_specs=placed, out_specs=(P("row", "col"), P(), P()), check_vma=False
    )
```

```python
import functools
import math

import jax
import jax.numpy as jnp
from jax import lax
from jax.experimental import pallas as pl
from jax.experimental.pallas import tpu as pltpu
from jax.sharding import PartitionSpec as P

BLK = 128
TB = 6
STEPS = 4
TILE = TB * BLK
WIDTH = 2 * BLK
TAIL = 16
LANES = 128
BOTH = ("row", "col")


def pack_kernel(left_slots, right_slots, left, right, left_out, right_out, held, table, read_sems, write_sems, tail_sems, slot_sems):
    depth = left.shape[0]
    part = depth // PARTS
    sides = ((left_slots, left, left_out), (right_slots, right, right_out))
    fetches = []
    for side, (slots, _, _) in enumerate(sides):
        fetches.append(pltpu.make_async_copy(slots, table.at[side], slot_sems.at[side]))
        fetches[-1].start()
    reads = []
    for side, (_, source, _) in enumerate(sides):
        for index in range(PARTS):
            rows = pl.ds(index * part, part)
            reads.append(pltpu.make_async_copy(source.at[rows], held.at[side, rows], read_sems.at[side, index]))
            reads[-1].start()
    lane = lax.broadcasted_iota(jnp.int32, (TAIL, LANES), 1)
    tail = pl.ds(depth, TAIL)
    writes = []
    for side, (slots, _, out) in enumerate(sides):
        fetches[side].wait()
        cells = jnp.zeros((TAIL, LANES), jnp.int32)
        for slot in range(slots.shape[1]):
            cells = jnp.where(lane == slot, table[side, 0, slot], cells)
        held[side, depth : depth + TAIL, :] = cells.astype(jnp.float32).astype(out.dtype)
        writes.append(pltpu.make_async_copy(held.at[side, tail], out.at[tail], tail_sems.at[side]))
        writes[-1].start()
    for side, (_, _, out) in enumerate(sides):
        for index in range(PARTS):
            rows = pl.ds(index * part, part)
            reads[side * PARTS + index].wait()
            writes.append(pltpu.make_async_copy(held.at[side, rows], out.at[rows], write_sems.at[side, index]))
            writes[-1].start()
    for copy in writes:
        copy.wait()


PARTS = 3


def pack(left_slots, right_slots, left, right):
    depth = left.shape[0]
    packed = jax.ShapeDtypeStruct((depth + TAIL, LANES), left.dtype)
    return pl.pallas_call(
        pack_kernel,
        out_shape=(packed, packed),
        in_specs=[pl.BlockSpec(memory_space=pl.ANY)] * 4,
        out_specs=(pl.BlockSpec(memory_space=pl.ANY),) * 2,
        scratch_shapes=[
            pltpu.VMEM((2, depth + TAIL, LANES), left.dtype),
            pltpu.SMEM((2,) + left_slots.shape, jnp.int32),
            pltpu.SemaphoreType.DMA((2, PARTS)),
            pltpu.SemaphoreType.DMA((2, PARTS)),
            pltpu.SemaphoreType.DMA((2,)),
            pltpu.SemaphoreType.DMA((2,)),
        ],
        name="pack_tiles",
    )(left_slots, right_slots, left, right)


def gather_cells(tiles, cells, table, sem):
    depth = tiles[0].shape[0] - TAIL
    level = lax.broadcasted_iota(jnp.int32, cells.shape, 0)
    gathered = jnp.zeros(cells.shape, jnp.int32)
    for index, tile in enumerate(tiles):
        tail = tile[depth : depth + TAIL, :].astype(jnp.float32).astype(jnp.int32)
        gathered = jnp.where(level == index, tail[0 : cells.shape[0]], gathered)
    cells[...] = gathered
    copy = pltpu.make_async_copy(cells, table, sem)
    copy.start()
    return copy


def place(tile, table, index, dense, base, side):
    for slot in range((tile.shape[0] - TAIL) // BLK):
        cell = table[index, slot]
        row, col = cell // TB * BLK, cell % TB * BLK
        if side == "left":
            col = base + col
        else:
            row = jnp.where(cell < TB * TB, base + row, dense.shape[0] - BLK)
        row, col = pl.multiple_of(row, BLK), pl.multiple_of(col, BLK)
        dense[pl.ds(row, BLK), pl.ds(col, BLK)] = tile[slot * BLK : (slot + 1) * BLK, :]


def first_kernel(left_0, right_0, left_1, right_1, accum, *scratches):
    left_dense, right_dense, cells, table, sem = scratches
    place_pairs((left_0, right_0, left_1, right_1), left_dense, right_dense, cells, table, sem)
    for low in range(0, TILE, WIDTH):
        accum[:, low : low + WIDTH] = multiply_pairs(left_dense, right_dense, low)


def place_kernel(left_2, right_2, left_dense, right_dense, cells, table, sem):
    place_pairs((left_2, right_2), left_dense, right_dense, cells, table, sem)


def last_kernel(on_diagonal, accum, left_early, right_early, left_3, right_3, out, sums, *scratches):
    left_dense, right_dense, cells, table, sem = scratches
    place_pairs((left_3, right_3), left_dense, right_dense, cells, table, sem)
    square_sum = jnp.float32(0)
    diagonal_sum = jnp.float32(0)
    inside = lax.broadcasted_iota(jnp.int32, (WIDTH, WIDTH), 0) == lax.broadcasted_iota(
        jnp.int32, (WIDTH, WIDTH), 1
    )
    for low in range(0, TILE, WIDTH):
        total = accum[:, low : low + WIDTH] + multiply_pairs(left_early, right_early, low)
        total += multiply_pairs(left_dense, right_dense, low)
        out[:, low : low + WIDTH] = total.astype(out.dtype)
        square_sum += jnp.sum(total * total)
        diagonal_sum += jnp.sum(jnp.where(inside, total[low : low + WIDTH, :], 0.0))
    diagonal_sum = jnp.where(on_diagonal[0] > 0, diagonal_sum, 0.0)
    lane = lax.broadcasted_iota(jnp.int32, sums.shape, 1)
    sums[...] = jnp.where(lane == 0, diagonal_sum, jnp.where(lane == 1, square_sum, 0.0))


def place_pairs(tiles, left_dense, right_dense, cells, table, sem):
    copy = gather_cells(tiles, cells, table, sem)
    left_dense[...] = jnp.zeros_like(left_dense)
    right_dense[...] = jnp.zeros_like(right_dense)
    copy.wait()
    for step in range(len(tiles) // 2):
        place(tiles[2 * step], table, 2 * step, left_dense, step * TILE, "left")
        place(tiles[2 * step + 1], table, 2 * step + 1, right_dense, step * TILE, "right")


def multiply_pairs(left_dense, right_dense, low):
    depth = left_dense.shape[1]
    return jnp.dot(
        left_dense[0:TILE, :],
        right_dense[0:depth, low : low + WIDTH],
        preferred_element_type=jnp.float32,
    )


WHOLE = pl.BlockSpec(memory_space=pltpu.VMEM)
CELLS = [pltpu.VMEM((8, LANES), jnp.int32), pltpu.SMEM((8, LANES), jnp.int32), pltpu.SemaphoreType.DMA]


def left_shape(steps):
    return (TILE + BLK, steps * TILE)


def right_shape(steps):
    return (steps * TILE + BLK, TILE)


def scratch(steps):
    return [pltpu.VMEM(left_shape(steps), jnp.bfloat16), pltpu.VMEM(right_shape(steps), jnp.bfloat16)] + CELLS


LIMIT = pltpu.CompilerParams(vmem_limit_bytes=14 * 2**20)
SMALL = pl.CostEstimate(flops=1000, bytes_accessed=1000, transcendentals=0)


def multiply(kernel, name, inputs, steps):
    return pl.pallas_call(
        kernel,
        out_shape=jax.ShapeDtypeStruct((TILE, TILE), jnp.float32),
        in_specs=[WHOLE] * len(inputs),
        out_specs=WHOLE,
        scratch_shapes=scratch(steps),
        compiler_params=LIMIT,
        cost_estimate=SMALL,
        name=name,
    )(*inputs)


def place_only(inputs):
    return pl.pallas_call(
        place_kernel,
        out_shape=(
            jax.ShapeDtypeStruct(left_shape(1), jnp.bfloat16),
            jax.ShapeDtypeStruct(right_shape(1), jnp.bfloat16),
        ),
        in_specs=[WHOLE] * 2,
        out_specs=(WHOLE, WHOLE),
        scratch_shapes=CELLS,
        compiler_params=LIMIT,
        cost_estimate=SMALL,
        name="place_forwarded",
    )(*inputs)


def multiply_last(on_diagonal, inputs, fan):
    return pl.pallas_call(
        last_kernel,
        out_shape=(
            jax.ShapeDtypeStruct((TILE, TILE), jnp.bfloat16),
            jax.ShapeDtypeStruct((fan, LANES), jnp.float32),
        ),
        in_specs=[pl.BlockSpec(memory_space=pltpu.SMEM)] + [WHOLE] * len(inputs),
        out_specs=(WHOLE, WHOLE),
        scratch_shapes=scratch(1),
        compiler_params=LIMIT,
        cost_estimate=SMALL,
        name="last_product",
    )(on_diagonal, *inputs)


def exchange(value, target, rows, cols):
    pairs = []
    for i in range(rows):
        for j in range(cols):
            to_row, to_col = target(i, j)
            pairs.append((i * cols + j, to_row % rows * cols + to_col % cols))
    return lax.ppermute(value, BOTH, pairs)


def spread_sum(values, axis):
    return lax.all_to_all(values, axis, 0, 0, tiled=True)


def body(left_blocks, left_slots, right_blocks, right_slots):
    rows, cols = lax.axis_size("row"), lax.axis_size("col")
    on_diagonal = (lax.axis_index("row") == lax.axis_index("col")).astype(jnp.int32).reshape(1)
    left, right = pack(
        left_slots, right_slots, left_blocks.reshape(-1, LANES), right_blocks.reshape(-1, LANES)
    )
    move = functools.partial(exchange, rows=rows, cols=cols)
    left_first = move(left, lambda i, j: (i, j - 1 if i % 2 == 0 else j - 3))
    left_second = move(left, lambda i, j: (i, j - 3 if i % 2 == 0 else j - 1))
    left_middle = move(left_first, lambda i, j: (i, j - 1 if i % 2 == 0 else j + 1))
    right_first = move(right, lambda i, j: (i - 1 if i % 2 else i - 3, j))
    right_middle = move(right, lambda i, j: (i - 2, j))
    accum = multiply(first_kernel, "first_products", (left, right, left_first, right_first), 2)
    right_middle, accum = lax.optimization_barrier((right_middle, accum))
    right_second = move(right_middle, lambda i, j: (i ^ 1, j))
    placed = place_only((left_middle, right_middle))
    product, partial = multiply_last(on_diagonal, (accum, *placed, left_second, right_second), rows)
    row_sums = jnp.sum(spread_sum(partial, "row"), axis=0, keepdims=True)
    totals = jnp.sum(spread_sum(jnp.broadcast_to(row_sums, (cols, LANES)), "col"), axis=0)
    trace_scaled = totals[0] / math.sqrt(min(rows, cols) * TILE)
    norm_scaled = totals[1] / (rows * cols * TILE * TILE)
    return product, trace_scaled, norm_scaled


def solution(mesh):
    placed = (
        P("row", "col", None, None),
        P("row", "col"),
        P("row", "col", None, None),
        P("row", "col"),
    )
    return jax.shard_map(
        body, mesh=mesh, in_specs=placed, out_specs=(P("row", "col"), P(), P()), check_vma=False
    )
```
